32 devices in a mesh: row: 4 (over y, x), col: 8 (over z, core).
Axes of the slice: x: 2, y: 2, z: 4, core: 2. Of those that a mesh axis runs over, the one named last changes fastest.
Arguments:
- sectors: int32 [96], replicated, may hold values from 0 to 7
- environment: bfloat16 [24576, 24576], P('col', 'row'), may hold values from -0.109375 to 0.109375
- wavefunction: bfloat16 [24576, 2048], P('row', 'col'), may hold values from -6 to 6
Outputs:
- applied: bfloat16 [24576, 2048], P('col', 'row')
The draws below stay inside these ranges and needn't reach their ends.
All inputs are finite; a program needn't handle non-finite values.
Results may differ from the reference program's by a relative error of at most 0.013.
Values may be sent and summed in bfloat16 or wider, within the bound.
No kernel may reach another device: no remote copies, remote signals or barrier semaphores. Data moves between devices by JAX's collectives and lax.ppermute only.
A program may use at most 192 MiB of HBM per device.

```python
import jax
import jax.numpy as jnp
from jax import lax

BOND = 24576
BLOCK = 256
COLS = 2048
SECTORS = 8
BLOCKS = 96


def place_ends(result, rng, smallest, high):
    shape = result.shape
    place = [jax.random.randint(jax.random.fold_in(rng, axis), (), 0, shape[axis]) for axis in range(len(shape))]
    result = result.at[tuple(place)].set(smallest)
    longest = shape.index(max(shape))
    place[longest] = (place[longest] + 1) % shape[longest]
    return result.at[tuple(place)].set(high)


def block_scale(stream_key, dims, shards, smallest, top_value):
    gain, own = 1.0, jax.random.fold_in(stream_key, 6)
    for axis_at, parts in shards:
        heights = jnp.exp(jax.random.uniform(jax.random.fold_in(own, axis_at), (parts,), jnp.float32, smallest / len(shards), top_value / len(shards)))
        gain = gain * jnp.repeat(heights, dims[axis_at] // parts).reshape([-1 if axis == axis_at else 1 for axis in range(len(dims))])
    return gain


def gaussian(stream_key, extent, scale, limit, split=(), kind=jnp.bfloat16):
    array = jax.random.normal(stream_key, extent, jnp.float32) * scale
    if len(split) > 0:
        array = block_scale(stream_key, extent, split, -0.22, 0.18) * array
    return jnp.clip(array, min=-limit, max=limit).astype(kind)


def setup_inputs(seed: int = 0) -> dict:
    key_list = jax.random.split(jax.random.key(seed), 4)
    sectors = place_ends(jax.random.randint(key_list[0], (BLOCKS,), 0, SECTORS), jax.random.fold_in(key_list[0], 1), 0, SECTORS - 1).astype(jnp.int32)
    environment = gaussian(key_list[1], (BOND, BOND), (BOND // SECTORS) ** -0.5, 0.109375, ((0, 8), (1, 4)))
    wavefunction = gaussian(key_list[2], (BOND, COLS), 1.0, 6.0, ((0, 4), (1, 8)))
    return dict(sectors=sectors, environment=environment, wavefunction=wavefunction)


def reference(sectors, environment, wavefunction):
    panels = environment.reshape(BLOCKS, BLOCK, BOND)

    def block_rows(pair):
        row_panel, sector = pair
        allowed = jnp.repeat(sectors == sector, BLOCK)
        masked = jnp.where(allowed[None, :], row_panel, jnp.zeros_like(row_panel))
        return jnp.dot(masked, wavefunction, preferred_element_type=jnp.float32).astype(jnp.bfloat16)

    stacked = lax.map(block_rows, (panels, sectors))
    return stacked.reshape(BOND, COLS)
```

```python
import functools

import jax
import jax.numpy as jnp
from jax import lax
from jax.experimental import pallas as pl
from jax.experimental.pallas import tpu as pltpu
from jax.sharding import PartitionSpec as P

BLOCK = 256
LANES = 128
SLOTS = 32
GROUP = 8
HIDING = 106 * 10**9
AXES = ("row", "col")
VMEM_BYTES = 60 * 1024 * 1024
TINY = pl.CostEstimate(flops=1, bytes_accessed=1, transcendentals=0)
TOKEN = jax.ShapeDtypeStruct((8, LANES), jnp.float32)
ANYWHERE = pl.BlockSpec(memory_space=pl.ANY)
SCALARS = pl.BlockSpec(memory_space=pltpu.SMEM)


def pair_kernel(row_blocks, col_blocks, bases_ref, sectors_ref, pairs_ref):
    def visit(step, count):
        i, j = step // col_blocks, step % col_blocks
        pairs_ref[1 + count] = i * 256 + j
        row = bases_ref[1 + i // row_blocks] + i % row_blocks
        same = sectors_ref[row] == sectors_ref[bases_ref[0] + j]
        return count + same.astype(jnp.int32)

    steps = (bases_ref.shape[0] - 1) * row_blocks * col_blocks
    pairs_ref[0] = lax.fori_loop(0, steps, visit, jnp.int32(0))


def block_pairs(sectors, row_blocks, col_blocks, cols):
    bases = jnp.stack([lax.axis_index("row") * col_blocks] + [col * row_blocks for col in cols]).astype(jnp.int32)
    return pl.pallas_call(
        functools.partial(pair_kernel, row_blocks, col_blocks),
        out_shape=jax.ShapeDtypeStruct((len(cols) * row_blocks * col_blocks + 1 + GROUP + SLOTS,), jnp.int32),
        in_specs=[SCALARS] * 2,
        out_specs=SCALARS,
        cost_estimate=TINY,
        name="block_pairs",
    )(bases, sectors)


def product_kernel(n_env, n_parts, n_old, n_out, writes, pairs_ref, at_ref, *refs):
    env_refs, part_refs = refs[:n_env], refs[n_env : n_env + 2 * n_parts]
    refs = refs[n_env + 2 * n_parts + n_old + 1 :]
    out_refs = refs[:n_out]
    wave, blocks, total, result, wave_sem, block_sem, out_sem = refs[n_out + 1 :]
    count = pairs_ref[0]
    row_blocks = env_refs[0].shape[0] // BLOCK

    def block_copy(step, env_ref, first):
        pair = pairs_ref[1 + step]
        rows = pl.ds(pl.multiple_of((pair // 256 - first) * BLOCK, BLOCK), BLOCK)
        source = env_ref.at[rows, pl.ds(pl.multiple_of(pair % 256 * BLOCK, BLOCK), BLOCK)]
        return pltpu.make_async_copy(source, blocks.at[step % SLOTS], block_sem.at[step % SLOTS])

    def fetch(step):
        i = pairs_ref[1 + step] // 256
        for n, env_ref in enumerate(env_refs):

            @pl.when((step < count) & (i >= n * row_blocks) & (i < (n + 1) * row_blocks))
            def _():
                block_copy(step, env_ref, n * row_blocks).start()

    waves, at = [], 0
    for k in range(n_parts):
        x_ref, y_ref = part_refs[2 * k : 2 * k + 2]
        target = wave.at[:, pl.ds(at, x_ref.shape[1])]
        waves.append(pltpu.make_async_copy(x_ref, target, wave_sem.at[k]))
        pl.when(at_ref[0] == 1)(waves[-1].start)
        pl.when(at_ref[0] == 0)(pltpu.make_async_copy(y_ref, target, wave_sem.at[k]).start)
        at += x_ref.shape[1]
    for step in range(SLOTS):
        fetch(step)

    total[...] = jnp.zeros_like(total)
    for copy in waves:
        copy.wait()

    spare = total.shape[0] // BLOCK - 1

    def visit(group, carry):
        steps = [group * GROUP + u for u in range(GROUP)]
        for step in steps:

            @pl.when(step < count)
            def _():
                source = env_refs[0].at[pl.ds(0, BLOCK), pl.ds(0, BLOCK)]
                pltpu.make_async_copy(source, blocks.at[step % SLOTS], block_sem.at[step % SLOTS]).wait()

        products = []
        for step in steps:
            real = step < count
            pair = pairs_ref[1 + step]
            i, j = jnp.where(real, pair // 256, spare), jnp.where(real, pair % 256, 0)
            rows = pl.ds(pl.multiple_of(i * BLOCK, BLOCK), BLOCK)
            depth = pl.ds(pl.multiple_of(j * BLOCK, BLOCK), BLOCK)
            products.append((rows, jnp.dot(blocks[step % SLOTS], wave[depth, :], preferred_element_type=jnp.float32)))
        for rows, product in products:
            total[rows, :] += product
        for step in steps:
            fetch(step + SLOTS)

        return carry

    lax.fori_loop(0, (count + GROUP - 1) // GROUP, visit, 0)
    result[...] = total[: result.shape[0], :].astype(result.dtype)
    copies = []
    for k, (start, size, top, height, target, tile) in enumerate(writes):
        there = pl.ds(pl.multiple_of(at_ref[tile], BLOCK) if tile else 0, height)
        source = result.at[pl.ds(top, height), pl.ds(start, size)]
        copies.append(pltpu.make_async_copy(source, out_refs[target].at[there, :], out_sem.at[k]))
        copies[-1].start()
    for copy in copies:
        copy.wait()


def block_product(pairs, at, environments, parts, old, new, writes, after, flops=1):
    rows, depth = environments[0].shape
    rows, width, n_env = rows * len(environments), sum(x.shape[1] for x, _ in parts), len(environments)
    results = pl.pallas_call(
        functools.partial(product_kernel, n_env, len(parts), len(old), len(old) + len(new), writes),
        out_shape=[jax.ShapeDtypeStruct(z.shape, z.dtype) for z in (*old, *new)] + [TOKEN],
        in_specs=[SCALARS] * 2 + [ANYWHERE] * (n_env + 2 * len(parts) + 1 + len(old)),
        out_specs=[ANYWHERE] * (len(old) + len(new) + 1),
        scratch_shapes=[
            pltpu.VMEM((depth, width), jnp.bfloat16),
            pltpu.VMEM((SLOTS, BLOCK, BLOCK), jnp.bfloat16),
            pltpu.VMEM((rows + BLOCK, width), jnp.float32),
            pltpu.VMEM((rows, width), jnp.bfloat16),
            pltpu.SemaphoreType.DMA((len(parts),)),
            pltpu.SemaphoreType.DMA((SLOTS,)),
            pltpu.SemaphoreType.DMA((len(writes),)),
        ],
        input_output_aliases={2 + n_env + 2 * len(parts) + k: k for k in range(len(old))},
        compiler_params=pltpu.CompilerParams(vmem_limit_bytes=VMEM_BYTES),
        cost_estimate=pl.CostEstimate(flops=flops, bytes_accessed=1, transcendentals=0),
        name="block_product",
    )(pairs, at, *environments, *(z for part in parts for z in part), *old, after)
    return results[:-1], results[-1]


def gate_kernel(*refs):
    del refs


def gate(held, after):
    out = pl.pallas_call(
        gate_kernel,
        out_shape=[jax.ShapeDtypeStruct(x.shape, x.dtype) for x in held] + [TOKEN],
        in_specs=[ANYWHERE] * (len(held) + len(after)),
        out_specs=[ANYWHERE] * (len(held) + 1),
        input_output_aliases={k: k for k in range(len(held))},
        compiler_params=pltpu.CompilerParams(vmem_limit_bytes=VMEM_BYTES),
        name="gate",
    )(*held, *after)
    return out[:-1], out[-1]


def add_kernel(count, *refs):
    pairs, outs = refs[: 2 * count], refs[2 * count + 1 : 3 * count + 1]
    held, sums, read_sem, write_sem = refs[3 * count + 2 :]
    reads = [pltpu.make_async_copy(ref, held.at[k], read_sem.at[k]) for k, ref in enumerate(pairs)]
    writes = [pltpu.make_async_copy(sums.at[k], ref, write_sem.at[k]) for k, ref in enumerate(outs)]
    for read in reads:
        read.start()
    for k, write in enumerate(writes):
        reads[2 * k].wait()
        reads[2 * k + 1].wait()
        sums[k] = (held[2 * k].astype(jnp.float32) + held[2 * k + 1].astype(jnp.float32)).astype(sums.dtype)
        write.start()
    for write in writes:
        write.wait()


def add_pairs(pairs, after, flops=1):
    count, shape = len(pairs), pairs[0][0].shape
    results = pl.pallas_call(
        functools.partial(add_kernel, count),
        out_shape=[jax.ShapeDtypeStruct(shape, jnp.bfloat16)] * count + [TOKEN],
        in_specs=[ANYWHERE] * (2 * count + 1),
        out_specs=[ANYWHERE] * (count + 1),
        scratch_shapes=[
            pltpu.VMEM((2 * count, *shape), jnp.bfloat16),
            pltpu.VMEM((count, *shape), jnp.bfloat16),
            pltpu.SemaphoreType.DMA((2 * count,)),
            pltpu.SemaphoreType.DMA((count,)),
        ],
        compiler_params=pltpu.CompilerParams(vmem_limit_bytes=VMEM_BYTES),
        cost_estimate=pl.CostEstimate(flops=flops, bytes_accessed=1, transcendentals=0),
        name="add_pairs",
    )(*(x for pair in pairs for x in pair), after)
    return results[:-1], results[-1]


def place_kernel(piece, count, flags_ref, *refs):
    pairs, out_ref = refs[: 2 * count], refs[2 * count + 2]
    held, sums, read_sem, write_sem = refs[2 * count + 4 :]
    width = pairs[0].shape[1]

    @pl.when(flags_ref[0] == 1)
    def _():
        reads = [pltpu.make_async_copy(ref, held.at[k], read_sem.at[k]) for k, ref in enumerate(pairs)]
        for read in reads:
            read.start()
        writes = []
        for k in range(count):
            reads[2 * k].wait()
            reads[2 * k + 1].wait()
            sums[k] = (held[2 * k].astype(jnp.float32) + held[2 * k + 1].astype(jnp.float32)).astype(sums.dtype)
            core = flags_ref[1] if k == 0 else 1 - flags_ref[1]
            at = pl.multiple_of(core * (out_ref.shape[1] // 2) + piece * width, LANES)
            writes.append(pltpu.make_async_copy(sums.at[k], out_ref.at[:, pl.ds(at, width)], write_sem.at[k]))
            writes[-1].start()
        for write in writes:
            write.wait()


def place(out, flags, piece, pairs, after):
    count, shape = len(pairs), pairs[0][0].shape
    return pl.pallas_call(
        functools.partial(place_kernel, piece, count),
        out_shape=[jax.ShapeDtypeStruct(out.shape, out.dtype), TOKEN],
        in_specs=[SCALARS] + [ANYWHERE] * (2 * count + 2),
        out_specs=[ANYWHERE] * 2,
        scratch_shapes=[
            pltpu.VMEM((2 * count, *shape), jnp.bfloat16),
            pltpu.VMEM((count, *shape), jnp.bfloat16),
            pltpu.SemaphoreType.DMA((2 * count,)),
            pltpu.SemaphoreType.DMA((count,)),
        ],
        input_output_aliases={1 + 2 * count: 0},
        compiler_params=pltpu.CompilerParams(vmem_limit_bytes=VMEM_BYTES),
        cost_estimate=TINY,
        name="place",
    )(flags, *(x for pair in pairs for x in pair), out, after)


def place_set_kernel(core_ref, own_ref, other_ref, old_ref, after_ref, out_ref, token_ref, held, read_sem, write_sem):
    del old_ref, after_ref, token_ref
    height, width = held.shape[1:]
    sources = (own_ref.at[pl.ds(0, height), :], other_ref)
    reads = [pltpu.make_async_copy(ref, held.at[k], read_sem.at[k]) for k, ref in enumerate(sources)]
    for read in reads:
        read.start()
    writes = []
    for k in range(2):
        reads[k].wait()
        core = core_ref[0] if k == 0 else 1 - core_ref[0]
        at = pl.multiple_of(core * (out_ref.shape[1] // 2), LANES)
        writes.append(pltpu.make_async_copy(held.at[k], out_ref.at[:, pl.ds(at, width)], write_sem.at[k]))
        writes[-1].start()
    for write in writes:
        write.wait()


def place_set(out, core, own, other, after):
    return pl.pallas_call(
        place_set_kernel,
        out_shape=[jax.ShapeDtypeStruct(out.shape, out.dtype), TOKEN],
        in_specs=[SCALARS] + [ANYWHERE] * 4,
        out_specs=[ANYWHERE] * 2,
        scratch_shapes=[
            pltpu.VMEM((2, *other.shape), other.dtype),
            pltpu.SemaphoreType.DMA((2,)),
            pltpu.SemaphoreType.DMA((2,)),
        ],
        input_output_aliases={3: 0},
        compiler_params=pltpu.CompilerParams(vmem_limit_bytes=VMEM_BYTES),
        cost_estimate=TINY,
        name="place_set",
    )(core, own, other, out, after)


def empty_kernel(out_ref):
    del out_ref


def empty(shape):
    return pl.pallas_call(
        empty_kernel,
        out_shape=jax.ShapeDtypeStruct(shape, jnp.bfloat16),
        out_specs=ANYWHERE,
        name="empty",
    )()


def line_body(n_row, n_col, sectors, environment, wavefunction):
    rows, depth = environment.shape
    planes = n_col // 2
    last = planes - 1
    ends = {0: 1, last: last - 1}

    def along_z(moves):
        return [(r * n_col + z * 2 + a, r * n_col + to * 2 + a) for r in range(n_row) for z, to in moves for a in range(2)]

    swap_pairs = along_z([(z, z ^ 1) for z in range(planes)])
    swap_middle = along_z([(1, 2), (2, 1)])
    to_ends = along_z([(1, 0), (2, 3)])
    swap_cores = [(d, d ^ 1) for d in range(n_row * n_col)]
    owners = [
        [z for z in range(planes)],
        [z ^ 1 for z in range(planes)],
        [2, 2, 1, 1],
        [3, 3, 0, 0],
    ]

    def in_plane(owner, moves):
        return [
            ((owner[z] ^ at) * n_col + z * 2 + a, (owner[z] ^ at ^ by) * n_col + z * 2 + a)
            for z in range(planes)
            for at, by in moves
            for a in range(2)
        ]

    def move(x, moves):
        return lax.ppermute(x, AXES, moves)

    row, col = lax.axis_index("row"), lax.axis_index("col")
    plane, core = col // 2, col % 2
    is_end = (plane == 0) | (plane == last)
    pairs = block_pairs(sectors, rows // BLOCK, depth // BLOCK, [col, col ^ 1])
    width = wavefunction.shape[1]
    part = width // 2
    local = [wavefunction[:, :part], wavefunction[:, part:]]
    summed = empty((n_row * 2 * rows, part))
    out = empty((rows, 2 * width))
    first, final = {}, {}
    half = [jax.ShapeDtypeStruct((rows, part), jnp.bfloat16)] * 2

    def into_set(start, tile):
        return [(start, part, 0, 2 * rows, 0, tile)]

    def into_halves(start, target):
        return [(start, part, k * rows, rows, target + k, 0) for k in range(2)]

    def product(granules, parts, old, new, writes, after):
        tiles = [jnp.asarray(owners[g])[plane] * 2 * rows for g in granules]
        at = jnp.stack([is_end, *tiles]).astype(jnp.int32)
        return block_product(pairs, at, both_rows, parts, old, new, writes, after)

    def first_step(g, made):
        ways = zip(made, (2, 1))
        first[g] = [(x, move(x, in_plane(owners[g], [(3, p), (p, p)]))) for x, p in ways]

    def second_step(g, after, flops=1):
        (own, other), token = add_pairs(first.pop(g), after, flops)
        across = [(a, b ^ 1) for a, b in in_plane(owners[g], [(2, 2)])]
        final[g] = [(own, move(own, in_plane(owners[g], [(1, 1)]))), (move(other, swap_cores), move(other, across))]
        return token

    def finish(g, out, after):
        mine = jnp.asarray(owners[g])[plane] == row
        flags = jnp.stack([mine, core]).astype(jnp.int32)
        return place(out, flags, 1, final.pop(g), after)

    nearest, middle, second, far, third = ([None, None] for _ in range(5))
    nearest[0], middle[0] = move(local[0], swap_pairs), move(local[0], swap_middle)
    nearest[1] = move(local[1], swap_pairs)
    both_rows = [environment, move(environment, swap_cores)]

    (nearest[0], middle[0]), token = gate([nearest[0], middle[0]], [pairs])
    second[0], far[0] = move(middle[0], to_ends), move(nearest[0], swap_middle)
    (nearest[1], far[0], late), token = gate([nearest[1], far[0], local[1]], [token])
    third[0], middle[1] = move(far[0], to_ends), move(late, swap_middle)

    writes = into_set(0, 1) + into_halves(part, 1)
    (summed, *made), token = product([0], [(wavefunction, wavefunction)], [summed], half, writes, token)
    first_step(0, made)
    parts = [(x, x) for x in nearest]
    (summed, *made), token = product([1], parts, [summed], half, writes, token)
    first_step(1, made)

    (second[0], middle[1]), token = gate([second[0], middle[1]], [token])
    far[1], second[1] = move(nearest[1], swap_middle), move(middle[1], to_ends)
    token = second_step(0, token)

    (third[0], far[1]), token = gate([third[0], far[1]], [token])
    third[1] = move(far[1], to_ends)
    parts = [(second[0], middle[0]), (third[0], far[0])]
    (summed,), token = product([2, 3], parts, [summed], [], into_set(0, 1) + into_set(part, 2), token)
    scattered = lax.psum_scatter(summed, "row", scatter_dimension=0, tiled=True)
    token = second_step(1, token)

    (second[1],), token = gate([second[1]], [token])
    made, token = product([], [(second[1], middle[1])], [], half, into_halves(0, 0), token)
    first_step(2, made)
    out, token = finish(0, out, token)
    out, token = finish(1, out, token)

    (third[1],), token = gate([third[1]], [token])
    made, token = product([], [(third[1], far[1])], [], half, into_halves(0, 0), token)
    first_step(3, made)
    token = second_step(2, token, HIDING)
    token = second_step(3, token)
    out, token = finish(2, out, token)
    other = move(scattered[rows:], swap_cores)
    out, token = place_set(out, core.astype(jnp.int32)[None], scattered, other, token)
    out, token = finish(3, out, token)
    return out


def gather_body(sectors, environment, wavefunction):
    rows, depth = environment.shape
    pairs = block_pairs(sectors, rows // BLOCK, depth // BLOCK, [lax.axis_index("col")])
    gathered = lax.all_gather(wavefunction, "col", axis=1, tiled=True)
    wide = gathered.shape[1]
    new, writes = jax.ShapeDtypeStruct((rows, wide), jnp.bfloat16), [(0, wide, 0, rows, 0, 0)]
    at = jnp.ones((1,), jnp.int32)
    (partial_value,), _ = block_product(pairs, at, [environment], [(gathered, gathered)], [], [new], writes, pairs)
    return lax.psum_scatter(partial_value, "row", scatter_dimension=1, tiled=True)


def solution(mesh):
    n_row, n_col = mesh.shape["row"], mesh.shape["col"]
    body = gather_body
    if n_row == 4 and n_col == 8:
        body = functools.partial(line_body, n_row, n_col)
    placed = (P(), P("col", "row"), P("row", "col"))
    return jax.shard_map(body, mesh=mesh, in_specs=placed, out_specs=P("col", "row"), check_vma=False)
```

```python
import functools

import jax
import jax.numpy as jnp
from jax import lax
from jax.experimental import pallas as pl
from jax.experimental.pallas import tpu as pltpu
from jax.sharding import PartitionSpec as P

BLOCK = 256
LANES = 128
SLOTS = 32
GROUP = 8
HIDING = 115 * 10**9
AXES = ("row", "col")
VMEM_BYTES = 60 * 1024 * 1024
TINY = pl.CostEstimate(flops=1, bytes_accessed=1, transcendentals=0)
TOKEN = jax.ShapeDtypeStruct((8, LANES), jnp.float32)
ANYWHERE = pl.BlockSpec(memory_space=pl.ANY)
SCALARS = pl.BlockSpec(memory_space=pltpu.SMEM)


def pair_kernel(row_blocks, col_blocks, bases_ref, sectors_ref, pairs_ref):
    def visit(step, count):
        i, j = step // col_blocks, step % col_blocks
        pairs_ref[1 + count] = i * 256 + j
        row = bases_ref[1 + i // row_blocks] + i % row_blocks
        same = sectors_ref[row] == sectors_ref[bases_ref[0] + j]
        return count + same.astype(jnp.int32)

    steps = (bases_ref.shape[0] - 1) * row_blocks * col_blocks
    pairs_ref[0] = lax.fori_loop(0, steps, visit, jnp.int32(0))


def block_pairs(sectors, row_blocks, col_blocks, cols):
    bases = jnp.stack([lax.axis_index("row") * col_blocks] + [col * row_blocks for col in cols]).astype(jnp.int32)
    return pl.pallas_call(
        functools.partial(pair_kernel, row_blocks, col_blocks),
        out_shape=jax.ShapeDtypeStruct((len(cols) * row_blocks * col_blocks + 1 + GROUP + SLOTS,), jnp.int32),
        in_specs=[SCALARS] * 2,
        out_specs=SCALARS,
        cost_estimate=TINY,
        name="block_pairs",
    )(bases, sectors)


def product_kernel(n_env, n_parts, n_old, n_out, writes, pairs_ref, at_ref, *refs):
    env_refs, part_refs = refs[:n_env], refs[n_env : n_env + 2 * n_parts]
    refs = refs[n_env + 2 * n_parts + n_old + 1 :]
    out_refs = refs[:n_out]
    wave, blocks, total, result, wave_sem, block_sem, out_sem = refs[n_out + 1 :]
    count = pairs_ref[0]
    row_blocks = env_refs[0].shape[0] // BLOCK

    def block_copy(step, env_ref, first):
        pair = pairs_ref[1 + step]
        rows = pl.ds(pl.multiple_of((pair // 256 - first) * BLOCK, BLOCK), BLOCK)
        source = env_ref.at[rows, pl.ds(pl.multiple_of(pair % 256 * BLOCK, BLOCK), BLOCK)]
        return pltpu.make_async_copy(source, blocks.at[step % SLOTS], block_sem.at[step % SLOTS])

    def fetch(step):
        i = pairs_ref[1 + step] // 256
        for n, env_ref in enumerate(env_refs):

            @pl.when((step < count) & (i >= n * row_blocks) & (i < (n + 1) * row_blocks))
            def _():
                block_copy(step, env_ref, n * row_blocks).start()

    waves, at = [], 0
    for k in range(n_parts):
        x_ref, y_ref = part_refs[2 * k : 2 * k + 2]
        target = wave.at[:, pl.ds(at, x_ref.shape[1])]
        waves.append(pltpu.make_async_copy(x_ref, target, wave_sem.at[k]))
        pl.when(at_ref[0] == 1)(waves[-1].start)
        pl.when(at_ref[0] == 0)(pltpu.make_async_copy(y_ref, target, wave_sem.at[k]).start)
        at += x_ref.shape[1]
    for step in range(SLOTS):
        fetch(step)

    total[...] = jnp.zeros_like(total)
    for copy in waves:
        copy.wait()

    spare = total.shape[0] // BLOCK - 1

    def visit(group, carry):
        steps = [group * GROUP + u for u in range(GROUP)]
        for step in steps:

            @pl.when(step < count)
            def _():
                source = env_refs[0].at[pl.ds(0, BLOCK), pl.ds(0, BLOCK)]
                pltpu.make_async_copy(source, blocks.at[step % SLOTS], block_sem.at[step % SLOTS]).wait()

        products = []
        for step in steps:
            real = step < count
            pair = pairs_ref[1 + step]
            i, j = jnp.where(real, pair // 256, spare), jnp.where(real, pair % 256, 0)
            rows = pl.ds(pl.multiple_of(i * BLOCK, BLOCK), BLOCK)
            depth = pl.ds(pl.multiple_of(j * BLOCK, BLOCK), BLOCK)
            products.append((rows, jnp.dot(blocks[step % SLOTS], wave[depth, :], preferred_element_type=jnp.float32)))
        for rows, product in products:
            total[rows, :] += product
        for step in steps:
            fetch(step + SLOTS)

        return carry

    lax.fori_loop(0, (count + GROUP - 1) // GROUP, visit, 0)
    result[...] = total[: result.shape[0], :].astype(result.dtype)
    copies = []
    for k, (start, size, top, height, target, tile) in enumerate(writes):
        there = pl.ds(pl.multiple_of(at_ref[tile], BLOCK) if tile else 0, height)
        source = result.at[pl.ds(top, height), pl.ds(start, size)]
        copies.append(pltpu.make_async_copy(source, out_refs[target].at[there, :], out_sem.at[k]))
        copies[-1].start()
    for copy in copies:
        copy.wait()


def block_product(pairs, at, environments, parts, old, new, writes, after, flops=1):
    rows, depth = environments[0].shape
    rows, width, n_env = rows * len(environments), sum(x.shape[1] for x, _ in parts), len(environments)
    results = pl.pallas_call(
        functools.partial(product_kernel, n_env, len(parts), len(old), len(old) + len(new), writes),
        out_shape=[jax.ShapeDtypeStruct(z.shape, z.dtype) for z in (*old, *new)] + [TOKEN],
        in_specs=[SCALARS] * 2 + [ANYWHERE] * (n_env + 2 * len(parts) + 1 + len(old)),
        out_specs=[ANYWHERE] * (len(old) + len(new) + 1),
        scratch_shapes=[
            pltpu.VMEM((depth, width), jnp.bfloat16),
            pltpu.VMEM((SLOTS, BLOCK, BLOCK), jnp.bfloat16),
            pltpu.VMEM((rows + BLOCK, width), jnp.float32),
            pltpu.VMEM((rows, width), jnp.bfloat16),
            pltpu.SemaphoreType.DMA((len(parts),)),
            pltpu.SemaphoreType.DMA((SLOTS,)),
            pltpu.SemaphoreType.DMA((len(writes),)),
        ],
        input_output_aliases={2 + n_env + 2 * len(parts) + k: k for k in range(len(old))},
        compiler_params=pltpu.CompilerParams(vmem_limit_bytes=VMEM_BYTES),
        cost_estimate=pl.CostEstimate(flops=flops, bytes_accessed=1, transcendentals=0),
        name="block_product",
    )(pairs, at, *environments, *(z for part in parts for z in part), *old, after)
    return results[:-1], results[-1]


def gate_kernel(*refs):
    del refs


def gate(held, after):
    out = pl.pallas_call(
        gate_kernel,
        out_shape=[jax.ShapeDtypeStruct(x.shape, x.dtype) for x in held] + [TOKEN],
        in_specs=[ANYWHERE] * (len(held) + len(after)),
        out_specs=[ANYWHERE] * (len(held) + 1),
        input_output_aliases={k: k for k in range(len(held))},
        compiler_params=pltpu.CompilerParams(vmem_limit_bytes=VMEM_BYTES),
        name="gate",
    )(*held, *after)
    return out[:-1], out[-1]


def add_kernel(count, parts, *refs):
    pairs, outs = refs[: 2 * count], refs[2 * count + 1 : (2 + parts) * count + 1]
    held, sums, read_sem, write_sem = refs[(2 + parts) * count + 2 :]
    high = sums.shape[1] // parts
    reads, writes = [], []
    for k in range(count * parts):
        rows = pl.ds(k % parts * high, high)
        for n in range(2):
            at = k // parts * 2 + n
            reads.append(pltpu.make_async_copy(pairs[at].at[rows, :], held.at[at, rows, :], read_sem.at[2 * k + n]))
            reads[-1].start()
        writes.append(pltpu.make_async_copy(sums.at[k // parts, rows, :], outs[k], write_sem.at[k]))
    for k, write in enumerate(writes):
        reads[2 * k].wait()
        reads[2 * k + 1].wait()
        rows, at = pl.ds(k % parts * high, high), k // parts
        both = held[2 * at, rows, :].astype(jnp.float32) + held[2 * at + 1, rows, :].astype(jnp.float32)
        sums[at, rows, :] = both.astype(sums.dtype)
        write.start()
    for write in writes:
        write.wait()


def add_pairs(pairs, after, flops=1, parts=1):
    count, shape = len(pairs), pairs[0][0].shape
    results = pl.pallas_call(
        functools.partial(add_kernel, count, parts),
        out_shape=[jax.ShapeDtypeStruct((shape[0] // parts, shape[1]), jnp.bfloat16)] * (count * parts) + [TOKEN],
        in_specs=[ANYWHERE] * (2 * count + 1),
        out_specs=[ANYWHERE] * (count * parts + 1),
        scratch_shapes=[
            pltpu.VMEM((2 * count, *shape), jnp.bfloat16),
            pltpu.VMEM((count, *shape), jnp.bfloat16),
            pltpu.SemaphoreType.DMA((2 * count * parts,)),
            pltpu.SemaphoreType.DMA((count * parts,)),
        ],
        compiler_params=pltpu.CompilerParams(vmem_limit_bytes=VMEM_BYTES),
        cost_estimate=pl.CostEstimate(flops=flops, bytes_accessed=1, transcendentals=0),
        name="add_pairs",
    )(*(x for pair in pairs for x in pair), after)
    return results[:-1], results[-1]


def place_kernel(piece, count, flags_ref, *refs):
    pairs, out_ref = refs[: 2 * count], refs[2 * count + 2]
    held, sums, read_sem, write_sem = refs[2 * count + 4 :]
    width = pairs[0].shape[1]

    @pl.when(flags_ref[0] == 1)
    def _():
        reads = [pltpu.make_async_copy(ref, held.at[k], read_sem.at[k]) for k, ref in enumerate(pairs)]
        for read in reads:
            read.start()
        writes = []
        for k in range(count):
            reads[2 * k].wait()
            reads[2 * k + 1].wait()
            sums[k] = (held[2 * k].astype(jnp.float32) + held[2 * k + 1].astype(jnp.float32)).astype(sums.dtype)
            core = flags_ref[1] if k == 0 else 1 - flags_ref[1]
            at = pl.multiple_of(core * (out_ref.shape[1] // 2) + piece * width, LANES)
            writes.append(pltpu.make_async_copy(sums.at[k], out_ref.at[:, pl.ds(at, width)], write_sem.at[k]))
            writes[-1].start()
        for write in writes:
            write.wait()


def place(out, flags, piece, pairs, after):
    count, shape = len(pairs), pairs[0][0].shape
    return pl.pallas_call(
        functools.partial(place_kernel, piece, count),
        out_shape=[jax.ShapeDtypeStruct(out.shape, out.dtype), TOKEN],
        in_specs=[SCALARS] + [ANYWHERE] * (2 * count + 2),
        out_specs=[ANYWHERE] * 2,
        scratch_shapes=[
            pltpu.VMEM((2 * count, *shape), jnp.bfloat16),
            pltpu.VMEM((count, *shape), jnp.bfloat16),
            pltpu.SemaphoreType.DMA((2 * count,)),
            pltpu.SemaphoreType.DMA((count,)),
        ],
        input_output_aliases={1 + 2 * count: 0},
        compiler_params=pltpu.CompilerParams(vmem_limit_bytes=VMEM_BYTES),
        cost_estimate=TINY,
        name="place",
    )(flags, *(x for pair in pairs for x in pair), out, after)


def place_set_kernel(piece, flags_ref, own_ref, other_ref, old_ref, after_ref, out_ref, token_ref, held, read_sem, write_sem):
    del old_ref, after_ref, token_ref
    height, width = held.shape[1:]

    @pl.when(flags_ref[0] == 1)
    def _():
        sources = (own_ref.at[pl.ds(0, height), :], other_ref)
        reads = [pltpu.make_async_copy(ref, held.at[k], read_sem.at[k]) for k, ref in enumerate(sources)]
        for read in reads:
            read.start()
        writes = []
        for k in range(2):
            reads[k].wait()
            core = flags_ref[1] if k == 0 else 1 - flags_ref[1]
            at = pl.multiple_of(core * (out_ref.shape[1] // 2) + piece * width, LANES)
            writes.append(pltpu.make_async_copy(held.at[k], out_ref.at[:, pl.ds(at, width)], write_sem.at[k]))
            writes[-1].start()
        for write in writes:
            write.wait()


def place_set(out, flags, piece, own, other, after):
    return pl.pallas_call(
        functools.partial(place_set_kernel, piece),
        out_shape=[jax.ShapeDtypeStruct(out.shape, out.dtype), TOKEN],
        in_specs=[SCALARS] + [ANYWHERE] * 4,
        out_specs=[ANYWHERE] * 2,
        scratch_shapes=[
            pltpu.VMEM((2, *other.shape), other.dtype),
            pltpu.SemaphoreType.DMA((2,)),
            pltpu.SemaphoreType.DMA((2,)),
        ],
        input_output_aliases={3: 0},
        compiler_params=pltpu.CompilerParams(vmem_limit_bytes=VMEM_BYTES),
        cost_estimate=TINY,
        name="place_set",
    )(flags, own, other, out, after)


def empty_kernel(out_ref):
    del out_ref


def empty(shape):
    return pl.pallas_call(
        empty_kernel,
        out_shape=jax.ShapeDtypeStruct(shape, jnp.bfloat16),
        out_specs=ANYWHERE,
        name="empty",
    )()


def line_body(n_row, n_col, sectors, environment, wavefunction):
    rows, depth = environment.shape
    planes = n_col // 2
    last = planes - 1
    ends = {0: 1, last: last - 1}

    def along_z(moves):
        return [(r * n_col + z * 2 + a, r * n_col + to * 2 + a) for r in range(n_row) for z, to in moves for a in range(2)]

    swap_pairs = along_z([(z, z ^ 1) for z in range(planes)])
    swap_middle = along_z([(1, 2), (2, 1)])
    to_ends = along_z([(1, 0), (2, 3)])
    swap_cores = [(d, d ^ 1) for d in range(n_row * n_col)]
    owners = [
        [z for z in range(planes)],
        [z ^ 1 for z in range(planes)],
        [2, 2, 1, 1],
        [3, 3, 0, 0],
    ]

    def in_plane(owner, moves):
        return [
            ((owner[z] ^ at) * n_col + z * 2 + a, (owner[z] ^ at ^ by) * n_col + z * 2 + a)
            for z in range(planes)
            for at, by in moves
            for a in range(2)
        ]

    def move(x, moves):
        return lax.ppermute(x, AXES, moves)

    row, col = lax.axis_index("row"), lax.axis_index("col")
    plane, core = col // 2, col % 2
    is_end = (plane == 0) | (plane == last)
    pairs = block_pairs(sectors, rows // BLOCK, depth // BLOCK, [col, col ^ 1])
    width = wavefunction.shape[1]
    part = width // 2
    local = [wavefunction[:, :part], wavefunction[:, part:]]
    summed = empty((n_row * 2 * rows, part))
    out = empty((rows, 2 * width))
    first, final = {}, {}
    half = [jax.ShapeDtypeStruct((rows, part), jnp.bfloat16)] * 2

    def into_set(start, tile):
        return [(start, part, 0, 2 * rows, 0, tile)]

    def into_halves(start, target):
        return [(start, part, k * rows, rows, target + k, 0) for k in range(2)]

    def product(granules, parts, old, new, writes, after):
        tiles = [jnp.asarray(owners[g])[plane] * 2 * rows for g in granules]
        at = jnp.stack([is_end, *tiles]).astype(jnp.int32)
        return block_product(pairs, at, both_rows, parts, old, new, writes, after)

    def first_step(g, made):
        ways = zip(made, (2, 1))
        first[g] = [(x, move(x, in_plane(owners[g], [(3, p), (p, p)]))) for x, p in ways]

    def second_step(g, after, flops=1):
        (own, other), token = add_pairs(first.pop(g), after, flops)
        across = [(a, b ^ 1) for a, b in in_plane(owners[g], [(2, 2)])]
        final[g] = [(own, move(own, in_plane(owners[g], [(1, 1)]))), (move(other, swap_cores), move(other, across))]
        return token

    def first_whole(g, made, p):
        first[g] = made, move(made, in_plane(owners[g], [(3, p), (p, p)]))

    def second_whole(g, q, after):
        (made,), token = add_pairs([first.pop(g)], after)
        final[g] = made, move(made, in_plane(owners[g], [(q, q)]))
        return token

    def add_whole(g, after):
        (own, other), token = add_pairs([final.pop(g)], after, 1, 2)
        final[g] = own, move(other, swap_cores)
        return token

    def flags(g):
        mine = jnp.asarray(owners[g])[plane] == row
        return jnp.stack([mine, core]).astype(jnp.int32)

    def finish_whole(g, out, after):
        return place_set(out, flags(g), 1, *final.pop(g), after)

    def finish(g, out, after):
        return place(out, flags(g), 1, final.pop(g), after)

    nearest, middle, second, far, third = ([None, None] for _ in range(5))
    nearest[0], middle[0] = move(local[0], swap_pairs), move(local[0], swap_middle)
    nearest[1] = move(local[1], swap_pairs)
    both_rows = [environment, move(environment, swap_cores)]

    (nearest[0], middle[0]), token = gate([nearest[0], middle[0]], [pairs])
    second[0], far[0] = move(middle[0], to_ends), move(nearest[0], swap_middle)
    (nearest[1], far[0], late), token = gate([nearest[1], far[0], local[1]], [token])
    third[0], middle[1] = move(far[0], to_ends), move(late, swap_middle)

    whole = [jax.ShapeDtypeStruct((2 * rows, part), jnp.bfloat16)]
    writes = into_set(0, 1) + [(part, part, 0, 2 * rows, 1, 0)]
    (summed, made), token = product([0], [(wavefunction, wavefunction)], [summed], whole, writes, token)
    first_whole(0, made, 2)
    (summed, made), token = product([1], [(x, x) for x in nearest], [summed], whole, writes, token)
    first_whole(1, made, 1)

    (second[0], middle[1]), token = gate([second[0], middle[1]], [token])
    far[1], second[1] = move(nearest[1], swap_middle), move(middle[1], to_ends)
    token = second_whole(0, 1, token)

    (third[0], far[1]), token = gate([third[0], far[1]], [token])
    third[1] = move(far[1], to_ends)
    parts = [(second[0], middle[0]), (third[0], far[0])]
    (summed,), token = product([2, 3], parts, [summed], [], into_set(0, 1) + into_set(part, 2), token)
    scattered = lax.psum_scatter(summed, "row", scatter_dimension=0, tiled=True)
    token = second_whole(1, 2, token)

    (second[1],), token = gate([second[1]], [token])
    made, token = product([], [(second[1], middle[1])], [], half, into_halves(0, 0), token)
    first_step(2, made)
    token = add_whole(0, token)

    (third[1],), token = gate([third[1]], [token])
    made, token = product([], [(third[1], far[1])], [], half, into_halves(0, 0), token)
    first_step(3, made)
    token = second_step(2, token, HIDING)
    token = add_whole(1, token)
    out, token = finish_whole(0, out, token)
    token = second_step(3, token)
    out, token = finish_whole(1, out, token)
    out, token = finish(2, out, token)
    other = move(scattered[rows:], swap_cores)
    everywhere = jnp.stack([jnp.ones_like(core), core]).astype(jnp.int32)
    out, token = place_set(out, everywhere, 0, scattered, other, token)
    out, token = finish(3, out, token)
    return out


def gather_body(sectors, environment, wavefunction):
    rows, depth = environment.shape
    pairs = block_pairs(sectors, rows // BLOCK, depth // BLOCK, [lax.axis_index("col")])
    gathered = lax.all_gather(wavefunction, "col", axis=1, tiled=True)
    wide = gathered.shape[1]
    new, writes = jax.ShapeDtypeStruct((rows, wide), jnp.bfloat16), [(0, wide, 0, rows, 0, 0)]
    at = jnp.ones((1,), jnp.int32)
    (partial_value,), _ = block_product(pairs, at, [environment], [(gathered, gathered)], [], [new], writes, pairs)
    return lax.psum_scatter(partial_value, "row", scatter_dimension=1, tiled=True)


def solution(mesh):
    n_row, n_col = mesh.shape["row"], mesh.shape["col"]
    body = gather_body
    if n_row == 4 and n_col == 8:
        body = functools.partial(line_body, n_row, n_col)
    placed = (P(), P("col", "row"), P("row", "col"))
    return jax.shard_map(body, mesh=mesh, in_specs=placed, out_specs=P("col", "row"), check_vma=False)
```

```python
import functools

import jax
import jax.numpy as jnp
from jax import lax
from jax.experimental import pallas as pl
from jax.experimental.pallas import tpu as pltpu
from jax.sharding import PartitionSpec as P

BLOCK = 256
LANES = 128
SLOTS = 32
GROUP = 8
HIDING = 115 * 10**9
AXES = ("row", "col")
VMEM_BYTES = 60 * 1024 * 1024
TINY = pl.CostEstimate(flops=1, bytes_accessed=1, transcendentals=0)
TOKEN = jax.ShapeDtypeStruct((8, LANES), jnp.float32)
ANYWHERE = pl.BlockSpec(memory_space=pl.ANY)
SCALARS = pl.BlockSpec(memory_space=pltpu.SMEM)


def pair_kernel(row_blocks, col_blocks, bases_ref, sectors_ref, pairs_ref):
    def visit(step, count):
        i, j = step // col_blocks, step % col_blocks
        pairs_ref[1 + count] = i * 256 + j
        row = bases_ref[1 + i // row_blocks] + i % row_blocks
        same = sectors_ref[row] == sectors_ref[bases_ref[0] + j]
        return count + same.astype(jnp.int32)

    steps = (bases_ref.shape[0] - 1) * row_blocks * col_blocks
    pairs_ref[0] = lax.fori_loop(0, steps, visit, jnp.int32(0))


def block_pairs(sectors, row_blocks, col_blocks, cols):
    bases = jnp.stack([lax.axis_index("row") * col_blocks] + [col * row_blocks for col in cols]).astype(jnp.int32)
    return pl.pallas_call(
        functools.partial(pair_kernel, row_blocks, col_blocks),
        out_shape=jax.ShapeDtypeStruct((len(cols) * row_blocks * col_blocks + 1 + GROUP + SLOTS,), jnp.int32),
        in_specs=[SCALARS] * 2,
        out_specs=SCALARS,
        cost_estimate=TINY,
        name="block_pairs",
    )(bases, sectors)


def product_kernel(n_env, n_parts, n_old, n_out, writes, pairs_ref, at_ref, *refs):
    env_refs, part_refs = refs[:n_env], refs[n_env : n_env + 2 * n_parts]
    refs = refs[n_env + 2 * n_parts + n_old + 1 :]
    out_refs = refs[:n_out]
    wave, blocks, total, result, wave_sem, block_sem, out_sem = refs[n_out + 1 :]
    count = pairs_ref[0]
    row_blocks = env_refs[0].shape[0] // BLOCK

    def block_copy(step, env_ref, first):
        pair = pairs_ref[1 + step]
        rows = pl.ds(pl.multiple_of((pair // 256 - first) * BLOCK, BLOCK), BLOCK)
        source = env_ref.at[rows, pl.ds(pl.multiple_of(pair % 256 * BLOCK, BLOCK), BLOCK)]
        return pltpu.make_async_copy(source, blocks.at[step % SLOTS], block_sem.at[step % SLOTS])

    def fetch(step):
        i = pairs_ref[1 + step] // 256
        for n, env_ref in enumerate(env_refs):

            @pl.when((step < count) & (i >= n * row_blocks) & (i < (n + 1) * row_blocks))
            def _():
                block_copy(step, env_ref, n * row_blocks).start()

    waves, at = [], 0
    for k in range(n_parts):
        x_ref, y_ref = part_refs[2 * k : 2 * k + 2]
        target = wave.at[:, pl.ds(at, x_ref.shape[1])]
        waves.append(pltpu.make_async_copy(x_ref, target, wave_sem.at[k]))
        pl.when(at_ref[0] == 1)(waves[-1].start)
        pl.when(at_ref[0] == 0)(pltpu.make_async_copy(y_ref, target, wave_sem.at[k]).start)
        at += x_ref.shape[1]
    for step in range(SLOTS):
        fetch(step)

    total[...] = jnp.zeros_like(total)
    for copy in waves:
        copy.wait()

    spare = total.shape[0] // BLOCK - 1

    def visit(group, carry):
        steps = [group * GROUP + u for u in range(GROUP)]
        for step in steps:

            @pl.when(step < count)
            def _():
                source = env_refs[0].at[pl.ds(0, BLOCK), pl.ds(0, BLOCK)]
                pltpu.make_async_copy(source, blocks.at[step % SLOTS], block_sem.at[step % SLOTS]).wait()

        products = []
        for step in steps:
            real = step < count
            pair = pairs_ref[1 + step]
            i, j = jnp.where(real, pair // 256, spare), jnp.where(real, pair % 256, 0)
            rows = pl.ds(pl.multiple_of(i * BLOCK, BLOCK), BLOCK)
            depth = pl.ds(pl.multiple_of(j * BLOCK, BLOCK), BLOCK)
            products.append((rows, jnp.dot(blocks[step % SLOTS], wave[depth, :], preferred_element_type=jnp.float32)))
        for rows, product in products:
            total[rows, :] += product
        for step in steps:
            fetch(step + SLOTS)

        return carry

    lax.fori_loop(0, (count + GROUP - 1) // GROUP, visit, 0)
    copies, ready = [], set()
    for k, (start, size, top, height, target, tile) in enumerate(writes):
        there = pl.ds(pl.multiple_of(at_ref[tile], BLOCK) if tile else 0, height)
        if (top, height) not in ready:
            result[top : top + height, :] = total[top : top + height, :].astype(result.dtype)
            ready.add((top, height))
        source = result.at[pl.ds(top, height), pl.ds(start, size)]
        copies.append(pltpu.make_async_copy(source, out_refs[target].at[there, :], out_sem.at[k]))
        copies[-1].start()
    for copy in copies:
        copy.wait()


def block_product(pairs, at, environments, parts, old, new, writes, after, flops=1):
    rows, depth = environments[0].shape
    rows, width, n_env = rows * len(environments), sum(x.shape[1] for x, _ in parts), len(environments)
    results = pl.pallas_call(
        functools.partial(product_kernel, n_env, len(parts), len(old), len(old) + len(new), writes),
        out_shape=[jax.ShapeDtypeStruct(z.shape, z.dtype) for z in (*old, *new)] + [TOKEN],
        in_specs=[SCALARS] * 2 + [ANYWHERE] * (n_env + 2 * len(parts) + 1 + len(old)),
        out_specs=[ANYWHERE] * (len(old) + len(new) + 1),
        scratch_shapes=[
            pltpu.VMEM((depth, width), jnp.bfloat16),
            pltpu.VMEM((SLOTS, BLOCK, BLOCK), jnp.bfloat16),
            pltpu.VMEM((rows + BLOCK, width), jnp.float32),
            pltpu.VMEM((rows, width), jnp.bfloat16),
            pltpu.SemaphoreType.DMA((len(parts),)),
            pltpu.SemaphoreType.DMA((SLOTS,)),
            pltpu.SemaphoreType.DMA((len(writes),)),
        ],
        input_output_aliases={2 + n_env + 2 * len(parts) + k: k for k in range(len(old))},
        compiler_params=pltpu.CompilerParams(vmem_limit_bytes=VMEM_BYTES),
        cost_estimate=pl.CostEstimate(flops=flops, bytes_accessed=1, transcendentals=0),
        name="block_product",
    )(pairs, at, *environments, *(z for part in parts for z in part), *old, after)
    return results[:-1], results[-1]


def gate_kernel(*refs):
    del refs


def gate(held, after):
    out = pl.pallas_call(
        gate_kernel,
        out_shape=[jax.ShapeDtypeStruct(x.shape, x.dtype) for x in held] + [TOKEN],
        in_specs=[ANYWHERE] * (len(held) + len(after)),
        out_specs=[ANYWHERE] * (len(held) + 1),
        input_output_aliases={k: k for k in range(len(held))},
        compiler_params=pltpu.CompilerParams(vmem_limit_bytes=VMEM_BYTES),
        name="gate",
    )(*held, *after)
    return out[:-1], out[-1]


def add_kernel(count, parts, *refs):
    pairs, outs = refs[: 2 * count], refs[2 * count + 1 : (2 + parts) * count + 1]
    held, sums, read_sem, write_sem = refs[(2 + parts) * count + 2 :]
    high = sums.shape[1] // parts
    reads, writes = [], []
    for k in range(count * parts):
        rows = pl.ds(k % parts * high, high)
        for n in range(2):
            at = k // parts * 2 + n
            reads.append(pltpu.make_async_copy(pairs[at].at[rows, :], held.at[at, rows, :], read_sem.at[2 * k + n]))
            reads[-1].start()
        writes.append(pltpu.make_async_copy(sums.at[k // parts, rows, :], outs[k], write_sem.at[k]))
    for k, write in enumerate(writes):
        reads[2 * k].wait()
        reads[2 * k + 1].wait()
        rows, at = pl.ds(k % parts * high, high), k // parts
        both = held[2 * at, rows, :].astype(jnp.float32) + held[2 * at + 1, rows, :].astype(jnp.float32)
        sums[at, rows, :] = both.astype(sums.dtype)
        write.start()
    for write in writes:
        write.wait()


def add_pairs(pairs, after, flops=1, parts=1):
    count, shape = len(pairs), pairs[0][0].shape
    results = pl.pallas_call(
        functools.partial(add_kernel, count, parts),
        out_shape=[jax.ShapeDtypeStruct((shape[0] // parts, shape[1]), jnp.bfloat16)] * (count * parts) + [TOKEN],
        in_specs=[ANYWHERE] * (2 * count + 1),
        out_specs=[ANYWHERE] * (count * parts + 1),
        scratch_shapes=[
            pltpu.VMEM((2 * count, *shape), jnp.bfloat16),
            pltpu.VMEM((count, *shape), jnp.bfloat16),
            pltpu.SemaphoreType.DMA((2 * count * parts,)),
            pltpu.SemaphoreType.DMA((count * parts,)),
        ],
        compiler_params=pltpu.CompilerParams(vmem_limit_bytes=VMEM_BYTES),
        cost_estimate=pl.CostEstimate(flops=flops, bytes_accessed=1, transcendentals=0),
        name="add_pairs",
    )(*(x for pair in pairs for x in pair), after)
    return results[:-1], results[-1]


def place_kernel(piece, count, flags_ref, *refs):
    pairs, out_ref = refs[: 2 * count], refs[2 * count + 2]
    held, sums, read_sem, write_sem = refs[2 * count + 4 :]
    width = pairs[0].shape[1]

    @pl.when(flags_ref[0] == 1)
    def _():
        reads = [pltpu.make_async_copy(ref, held.at[k], read_sem.at[k]) for k, ref in enumerate(pairs)]
        for read in reads:
            read.start()
        writes = []
        for k in range(count):
            reads[2 * k].wait()
            reads[2 * k + 1].wait()
            sums[k] = (held[2 * k].astype(jnp.float32) + held[2 * k + 1].astype(jnp.float32)).astype(sums.dtype)
            core = flags_ref[1] if k == 0 else 1 - flags_ref[1]
            at = pl.multiple_of(core * (out_ref.shape[1] // 2) + piece * width, LANES)
            writes.append(pltpu.make_async_copy(sums.at[k], out_ref.at[:, pl.ds(at, width)], write_sem.at[k]))
            writes[-1].start()
        for write in writes:
            write.wait()


def place(out, flags, piece, pairs, after):
    count, shape = len(pairs), pairs[0][0].shape
    return pl.pallas_call(
        functools.partial(place_kernel, piece, count),
        out_shape=[jax.ShapeDtypeStruct(out.shape, out.dtype), TOKEN],
        in_specs=[SCALARS] + [ANYWHERE] * (2 * count + 2),
        out_specs=[ANYWHERE] * 2,
        scratch_shapes=[
            pltpu.VMEM((2 * count, *shape), jnp.bfloat16),
            pltpu.VMEM((count, *shape), jnp.bfloat16),
            pltpu.SemaphoreType.DMA((2 * count,)),
            pltpu.SemaphoreType.DMA((count,)),
        ],
        input_output_aliases={1 + 2 * count: 0},
        compiler_params=pltpu.CompilerParams(vmem_limit_bytes=VMEM_BYTES),
        cost_estimate=TINY,
        name="place",
    )(flags, *(x for pair in pairs for x in pair), out, after)


def place_set_kernel(piece, flags_ref, own_ref, other_ref, old_ref, after_ref, out_ref, token_ref, held, read_sem, write_sem):
    del old_ref, after_ref, token_ref
    height, width = held.shape[1:]

    @pl.when(flags_ref[0] == 1)
    def _():
        sources = (own_ref.at[pl.ds(0, height), :], other_ref)
        reads = [pltpu.make_async_copy(ref, held.at[k], read_sem.at[k]) for k, ref in enumerate(sources)]
        for read in reads:
            read.start()
        writes = []
        for k in range(2):
            reads[k].wait()
            core = flags_ref[1] if k == 0 else 1 - flags_ref[1]
            at = pl.multiple_of(core * (out_ref.shape[1] // 2) + piece * width, LANES)
            writes.append(pltpu.make_async_copy(held.at[k], out_ref.at[:, pl.ds(at, width)], write_sem.at[k]))
            writes[-1].start()
        for write in writes:
            write.wait()


def place_set(out, flags, piece, own, other, after):
    return pl.pallas_call(
        functools.partial(place_set_kernel, piece),
        out_shape=[jax.ShapeDtypeStruct(out.shape, out.dtype), TOKEN],
        in_specs=[SCALARS] + [ANYWHERE] * 4,
        out_specs=[ANYWHERE] * 2,
        scratch_shapes=[
            pltpu.VMEM((2, *other.shape), other.dtype),
            pltpu.SemaphoreType.DMA((2,)),
            pltpu.SemaphoreType.DMA((2,)),
        ],
        input_output_aliases={3: 0},
        compiler_params=pltpu.CompilerParams(vmem_limit_bytes=VMEM_BYTES),
        cost_estimate=TINY,
        name="place_set",
    )(flags, own, other, out, after)


def empty_kernel(out_ref):
    del out_ref


def empty(shape):
    return pl.pallas_call(
        empty_kernel,
        out_shape=jax.ShapeDtypeStruct(shape, jnp.bfloat16),
        out_specs=ANYWHERE,
        name="empty",
    )()


def line_body(n_row, n_col, sectors, environment, wavefunction):
    rows, depth = environment.shape
    planes = n_col // 2
    last = planes - 1
    ends = {0: 1, last: last - 1}

    def along_z(moves):
        return [(r * n_col + z * 2 + a, r * n_col + to * 2 + a) for r in range(n_row) for z, to in moves for a in range(2)]

    swap_pairs = along_z([(z, z ^ 1) for z in range(planes)])
    swap_middle = along_z([(1, 2), (2, 1)])
    to_ends = along_z([(1, 0), (2, 3)])
    swap_cores = [(d, d ^ 1) for d in range(n_row * n_col)]
    owners = [
        [z for z in range(planes)],
        [z ^ 1 for z in range(planes)],
        [2, 2, 1, 1],
        [3, 3, 0, 0],
    ]

    def in_plane(owner, moves):
        return [
            ((owner[z] ^ at) * n_col + z * 2 + a, (owner[z] ^ at ^ by) * n_col + z * 2 + a)
            for z in range(planes)
            for at, by in moves
            for a in range(2)
        ]

    def move(x, moves):
        return lax.ppermute(x, AXES, moves)

    row, col = lax.axis_index("row"), lax.axis_index("col")
    plane, core = col // 2, col % 2
    is_end = (plane == 0) | (plane == last)
    pairs = block_pairs(sectors, rows // BLOCK, depth // BLOCK, [col, col ^ 1])
    width = wavefunction.shape[1]
    part = width // 2
    local = [wavefunction[:, :part], wavefunction[:, part:]]
    summed = empty((n_row * 2 * rows, part))
    out = empty((rows, 2 * width))
    first, final = {}, {}
    half = [jax.ShapeDtypeStruct((rows, part), jnp.bfloat16)] * 2

    def into_set(start, tile):
        return [(start, part, 0, 2 * rows, 0, tile)]

    def into_halves(start, target):
        return [(start, part, k * rows, rows, target + k, 0) for k in range(2)]

    def product(granules, parts, old, new, writes, after):
        tiles = [jnp.asarray(owners[g])[plane] * 2 * rows for g in granules]
        at = jnp.stack([is_end, *tiles]).astype(jnp.int32)
        return block_product(pairs, at, both_rows, parts, old, new, writes, after)

    def first_step(g, made):
        ways = zip(made, (2, 1))
        first[g] = [(x, move(x, in_plane(owners[g], [(3, p), (p, p)]))) for x, p in ways]

    def second_step(g, after, flops=1):
        (own, other), token = add_pairs(first.pop(g), after, flops)
        across = [(a, b ^ 1) for a, b in in_plane(owners[g], [(2, 2)])]
        final[g] = [(own, move(own, in_plane(owners[g], [(1, 1)]))), (move(other, swap_cores), move(other, across))]
        return token

    def first_whole(g, made, p):
        first[g] = made, move(made, in_plane(owners[g], [(3, p), (p, p)]))

    def second_whole(g, q, after):
        (made,), token = add_pairs([first.pop(g)], after)
        final[g] = made, move(made, in_plane(owners[g], [(q, q)]))
        return token

    def add_whole(g, after):
        (own, other), token = add_pairs([final.pop(g)], after, 1, 2)
        final[g] = own, move(other, swap_cores)
        return token

    def flags(g):
        mine = jnp.asarray(owners[g])[plane] == row
        return jnp.stack([mine, core]).astype(jnp.int32)

    def finish_whole(g, out, after):
        return place_set(out, flags(g), 1, *final.pop(g), after)

    def finish(g, out, after):
        return place(out, flags(g), 1, final.pop(g), after)

    nearest, middle, second, far, third = ([None, None] for _ in range(5))
    nearest[0], middle[0] = move(local[0], swap_pairs), move(local[0], swap_middle)
    nearest[1] = move(local[1], swap_pairs)
    both_rows = [environment, move(environment, swap_cores)]

    (nearest[0], middle[0]), token = gate([nearest[0], middle[0]], [pairs])
    second[0], far[0] = move(middle[0], to_ends), move(nearest[0], swap_middle)
    (nearest[1], far[0], late), token = gate([nearest[1], far[0], local[1]], [token])
    third[0], middle[1] = move(far[0], to_ends), move(late, swap_middle)

    whole = [jax.ShapeDtypeStruct((2 * rows, part), jnp.bfloat16)]
    writes = into_set(0, 1) + [(part, part, 0, 2 * rows, 1, 0)]
    (summed, made), token = product([0], [(wavefunction, wavefunction)], [summed], whole, writes, token)
    first_whole(0, made, 2)
    (summed, made), token = product([1], [(x, x) for x in nearest], [summed], whole, writes, token)
    first_whole(1, made, 1)

    (second[0], middle[1]), token = gate([second[0], middle[1]], [token])
    far[1], second[1] = move(nearest[1], swap_middle), move(middle[1], to_ends)
    token = second_whole(0, 1, token)

    (third[0], far[1]), token = gate([third[0], far[1]], [token])
    third[1] = move(far[1], to_ends)
    parts = [(second[0], middle[0]), (third[0], far[0])]
    (summed,), token = product([2, 3], parts, [summed], [], into_set(0, 1) + into_set(part, 2), token)
    scattered = lax.psum_scatter(summed, "row", scatter_dimension=0, tiled=True)
    token = second_whole(1, 2, token)

    (second[1],), token = gate([second[1]], [token])
    made, token = product([], [(second[1], middle[1])], [], half, into_halves(0, 0), token)
    first_step(2, made)
    token = add_whole(0, token)

    (third[1],), token = gate([third[1]], [token])
    made, token = product([], [(third[1], far[1])], [], half, into_halves(0, 0), token)
    first_step(3, made)
    token = second_step(2, token, HIDING)
    token = add_whole(1, token)
    out, token = finish_whole(0, out, token)
    token = second_step(3, token)
    out, token = finish_whole(1, out, token)
    out, token = finish(2, out, token)
    other = move(scattered[rows:], swap_cores)
    everywhere = jnp.stack([jnp.ones_like(core), core]).astype(jnp.int32)
    out, token = place_set(out, everywhere, 0, scattered, other, token)
    out, token = finish(3, out, token)
    return out


def gather_body(sectors, environment, wavefunction):
    rows, depth = environment.shape
    pairs = block_pairs(sectors, rows // BLOCK, depth // BLOCK, [lax.axis_index("col")])
    gathered = lax.all_gather(wavefunction, "col", axis=1, tiled=True)
    wide = gathered.shape[1]
    new, writes = jax.ShapeDtypeStruct((rows, wide), jnp.bfloat16), [(0, wide, 0, rows, 0, 0)]
    at = jnp.ones((1,), jnp.int32)
    (partial_value,), _ = block_product(pairs, at, [environment], [(gathered, gathered)], [], [new], writes, pairs)
    return lax.psum_scatter(partial_value, "row", scatter_dimension=1, tiled=True)


def solution(mesh):
    n_row, n_col = mesh.shape["row"], mesh.shape["col"]
    body = gather_body
    if n_row == 4 and n_col == 8:
        body = functools.partial(line_body, n_row, n_col)
    placed = (P(), P("col", "row"), P("row", "col"))
    return jax.shard_map(body, mesh=mesh, in_specs=placed, out_specs=P("col", "row"), check_vma=False)
```
